256 devices in a mesh: dp: 32 (over x, z_hi, core), tensor: 8 (over y, z_lo).
Axes of the slice: x: 4, y: 4, z: 8 (z_hi: 4, z_lo: 2; z = z_hi * 2 + z_lo), core: 2. Of those that a mesh axis runs over, the one named last changes fastest.
Arguments:
- hidden: bfloat16 [16384, 8192], P(('dp', 'tensor')), may hold values from -6 to 6
- norm_gain: float32 [8192], replicated, may hold values from 0.1 to 1.9
- w_query: bfloat16 [8192, 8192], P('dp', 'tensor'), may hold values from -0.0625 to 0.0625
- w_key: bfloat16 [8192, 1024], P('dp', 'tensor'), may hold values from -0.0625 to 0.0625
- w_value: bfloat16 [8192, 1024], P('dp', 'tensor'), may hold values from -0.0625 to 0.0625
- d_query: bfloat16 [16384, 8192], P('dp', 'tensor'), may hold values from -12 to 12
- d_key: bfloat16 [16384, 1024], P('dp', 'tensor'), may hold values from -12 to 12
- d_value: bfloat16 [16384, 1024], P('dp', 'tensor'), may hold values from -12 to 12
- lengths: int32 [64], P('dp'), may hold values from 64 to 256, as said below
- proj_in: bfloat16 [8192, 64], replicated, may hold values from -0.0625 to 0.0625
- proj_query: bfloat16 [8192, 64], P('tensor'), may hold values from -0.0625 to 0.0625
- proj_key: bfloat16 [1024, 64], P('tensor'), may hold values from -0.1875 to 0.1875
- proj_value: bfloat16 [1024, 64], P('tensor'), may hold values from -0.1875 to 0.1875
- queries: bfloat16 [32768, 12288], P(('dp', 'tensor')), may hold values from -0.0034179688 to 0.0034179688
Outputs:
- scores: float32 [64, 32768], P(None, ('dp', 'tensor'))
- grad_hidden: bfloat16 [16384, 8192], P(('dp', 'tensor'))
The draws below stay inside these ranges and needn't reach their ends.
Inputs may be any that keep to these rules, and one draw needn't show every extreme that they name: lengths[e] counts the live leading tokens of sequence e among its 256 positions; the rest is padding.
All inputs are finite; a program needn't handle non-finite values.
Results may differ from the reference program's by a relative error of at most 0.02.
Values may be sent and summed in bfloat16 or wider, within the bound.
No kernel may reach another device: no remote copies, remote signals or barrier semaphores. Data moves between devices by JAX's collectives and lax.ppermute only.
A program may use at most 128 MiB of HBM per device.

```python
import jax
import jax.numpy as jnp
from jax import lax

D = 8192
R = 64
LEN = 256
QW = 8192
KW = 1024
FEAT = 12288
EXAMPLES = 64
TOKENS = 16384
QUERIES = 32768
N_TENSOR = 8


def draw_lengths(key, part):
    key = jax.random.fold_in(key, 7)
    drawn = jax.random.randint(key, (EXAMPLES,), LEN // 4, LEN + 1, dtype=jnp.int32)
    drawn = drawn.at[0].set(LEN)
    return drawn.at[EXAMPLES - 1].set(LEN // 4)


def with_spikes(entries, stream_key, source, target, blocks, factor):
    owner, partner = [(jnp.arange(entries.shape[axis_at]) // (entries.shape[axis_at] // blocks)).reshape([-1 if axis == axis_at else 1 for axis in range(entries.ndim)]) for axis_at in (source, target)]
    chosen = jax.random.permutation(stream_key, blocks)[partner]
    strong = (owner == chosen) | (owner == (partner + blocks // 2) % blocks)
    return jnp.where(strong, factor * entries, entries)


def shard_levels(stream_key, extent, split, low, top_value):
    gain, own = 1.0, jax.random.fold_in(stream_key, 6)
    for axis_at, parts in split:
        heights = jnp.exp(jax.random.uniform(jax.random.fold_in(own, axis_at), (parts,), jnp.float32, low / len(split), top_value / len(split)))
        gain = gain * jnp.repeat(heights, extent[axis_at] // parts).reshape([-1 if axis == axis_at else 1 for axis in range(len(extent))])
    return gain


def scatter_about(rng, dims, scale, most, shards=(), kind=jnp.bfloat16):
    entries = scale * jax.random.normal(rng, dims, jnp.float32)
    if shards:
        entries = entries * shard_levels(rng, dims, shards, -0.22, 0.18)
    return jnp.clip(entries, -most, most).astype(kind)


def bell_draw_with(own_key, shape, spread, limit, cuts, heavy, kind=jnp.bfloat16):
    values = spread * jax.random.normal(own_key, shape, jnp.float32)
    if cuts:
        values = values * shard_levels(own_key, shape, cuts, -0.22, 0.18)
    return jnp.clip(with_spikes(values, jax.random.fold_in(own_key, 3), *heavy), -limit, limit).astype(kind)


def setup_inputs(seed: int = 0) -> dict:
    key_of = jax.random.split(jax.random.key(seed), 15)
    return {
        "hidden": scatter_about(key_of[0], (TOKENS, D), 1.0, 6.0, ((0, 256),)),
        "norm_gain": jnp.clip(1.0 + 0.18 * jax.random.normal(key_of[1], (D,), jnp.float32), 0.1, 1.9),
        "w_query": scatter_about(key_of[2], (D, QW), D ** -0.5, 0.0625, ((0, 32), (1, 8))),
        "w_key": scatter_about(key_of[3], (D, KW), D ** -0.5, 0.0625, ((0, 32), (1, 8))),
        "w_value": scatter_about(key_of[4], (D, KW), D ** -0.5, 0.0625, ((0, 32), (1, 8))),
        "d_query": bell_draw_with(key_of[5], (TOKENS, QW), 2.0, 12.0, ((0, 32), (1, 8)), (1, 0, 32, 2.75)),
        "d_key": scatter_about(key_of[6], (TOKENS, KW), 2.0, 12.0, ((0, 32), (1, 8))),
        "d_value": scatter_about(key_of[7], (TOKENS, KW), 2.0, 12.0, ((0, 32), (1, 8))),
        "lengths": draw_lengths(jax.random.fold_in(key_of[14], 71), 0),
        "proj_in": scatter_about(key_of[9], (D, R), D ** -0.5, 0.0625),
        "proj_query": scatter_about(key_of[10], (QW, R), QW ** -0.5, 0.0625, ((0, 8),)),
        "proj_key": scatter_about(key_of[11], (KW, R), KW ** -0.5, 0.1875, ((0, 8),)),
        "proj_value": scatter_about(key_of[12], (KW, R), KW ** -0.5, 0.1875, ((0, 8),)),
        "queries": scatter_about(key_of[13], (QUERIES, FEAT), (3 * R * R * LEN) ** -0.5, 0.0034179688, ((0, 256),)),
    }


EPSILON = 1e-05

def block_term(grads, weights, start, count):
    left = grads[:, start:start + count]
    right = weights[:, start:start + count]
    return lax.dot_general(left, right, (((1,), (1,)), ((), ())), preferred_element_type=jnp.float32)

def reference(hidden, norm_gain, w_query, w_key, w_value, d_query, d_key, d_value, lengths, proj_in, proj_query, proj_key, proj_value, queries):
    rows32 = hidden.astype(jnp.float32)
    inv_rms = lax.rsqrt(lax.optimization_barrier(jnp.mean(rows32 * rows32, axis=1, keepdims=True)) + EPSILON)
    unit = rows32 * inv_rms
    normed = (unit * norm_gain).astype(jnp.bfloat16)
    query_cols = w_query.shape[1] // N_TENSOR
    key_cols = w_key.shape[1] // N_TENSOR
    input_grad = jnp.zeros(hidden.shape, jnp.float32)
    for block in range(N_TENSOR):
        term = block_term(d_query, w_query, block * query_cols, query_cols)
        term = term + block_term(d_key, w_key, block * key_cols, key_cols)
        term = term + block_term(d_value, w_value, block * key_cols, key_cols)
        rounded = lax.optimization_barrier(term.astype(jnp.bfloat16))
        input_grad = input_grad + rounded.astype(jnp.float32)
    gained = input_grad * norm_gain
    grad_hidden = (inv_rms * (gained - unit * lax.optimization_barrier(jnp.mean(gained * unit, axis=1, keepdims=True)))).astype(jnp.bfloat16)
    token_sketch = jnp.dot(normed, proj_in, preferred_element_type=jnp.float32).astype(jnp.bfloat16)
    head_sketch = jnp.stack([jnp.dot(d_query, proj_query, preferred_element_type=jnp.float32), jnp.dot(d_key, proj_key, preferred_element_type=jnp.float32), jnp.dot(d_value, proj_value, preferred_element_type=jnp.float32)], axis=1)
    rank = proj_in.shape[1]
    head_sketch = head_sketch.reshape(EXAMPLES, LEN, 3, rank)
    live = (lax.broadcasted_iota(jnp.int32, (EXAMPLES, LEN), 1) < lengths[:, None]).astype(jnp.float32)
    masked = head_sketch * live[:, :, None, None]
    inputs32 = token_sketch.astype(jnp.float32).reshape(EXAMPLES, LEN, rank)
    example_grad = jnp.einsum('sli,slmj->smij', inputs32, masked, precision=lax.Precision.HIGHEST)
    example_grad = example_grad.reshape(EXAMPLES, 3 * rank * rank).astype(jnp.bfloat16)
    scores = lax.dot_general(example_grad, queries, (((1,), (1,)), ((), ())), preferred_element_type=jnp.float32)
    return (scores, grad_hidden)
```

```python
import functools

import jax
import jax.numpy as jnp
from jax import lax
from jax.experimental import pallas as pl
from jax.experimental.pallas import tpu as pltpu
from jax.sharding import PartitionSpec as P

EPSILON = 1e-05
BF = jnp.bfloat16
F32 = jnp.float32
VMEM_LIMIT = 48 * 1024 * 1024

NX, NZ, NC, NY, NL = 4, 4, 2, 4, 2
TOK = 64


def along_x(v, step):
    return lax.ppermute(v, "dp", [(i, (i // 8 + step) % NX * 8 + i % 8) for i in range(32)])


def along_z(v, step):
    return lax.ppermute(
        v, "dp", [(i, i // 8 * 8 + (i // 2 + step) % NZ * 2 + i % 2) for i in range(32)]
    )


def other_core(v):
    return lax.ppermute(v, "dp", [(i, i ^ 1) for i in range(32)])


def along_y(v, step):
    return lax.ppermute(v, "tensor", [(t, (t // 2 + step) % NY * 2 + t % 2) for t in range(8)])


def swap_y(v, bits):
    return lax.ppermute(v, "tensor", [(t, t ^ (2 * bits)) for t in range(8)])


def swap_l(v):
    return lax.ppermute(v, "tensor", [(t, t ^ 1) for t in range(8)])


def prepare_kernel(where, dq, dk, dv, pq, pk, pv, cot, head):
    cot[:, :1024] = dq[...]
    cot[:, 1024:1152] = dk[...]
    cot[:, 1152:] = dv[...]
    head[:, :64] = jnp.dot(dq[...], pq[...], preferred_element_type=F32).astype(BF)
    head[:, 64:128] = jnp.dot(dk[...], pk[...], preferred_element_type=F32).astype(BF)
    head[:, 128:] = jnp.dot(dv[...], pv[...], preferred_element_type=F32).astype(BF)


def prepare(where, dq, dk, dv, pq, pk, pv):
    rows = lambda b, where: (where[b], 0)
    whole = lambda b, where: (0, 0)
    place = lambda b, where: (b, 0)
    return pl.pallas_call(
        prepare_kernel,
        grid_spec=pltpu.PrefetchScalarGridSpec(
            num_scalar_prefetch=1,
            grid=(8,),
            in_specs=[
                pl.BlockSpec((TOK, 1024), rows),
                pl.BlockSpec((TOK, 128), rows),
                pl.BlockSpec((TOK, 128), rows),
                pl.BlockSpec((1024, 64), whole),
                pl.BlockSpec((128, 64), whole),
                pl.BlockSpec((128, 64), whole),
            ],
            out_specs=[pl.BlockSpec((TOK, 1280), place), pl.BlockSpec((TOK, 192), place)],
        ),
        out_shape=[
            jax.ShapeDtypeStruct((512, 1280), BF),
            jax.ShapeDtypeStruct((512, 192), BF),
        ],
        compiler_params=pltpu.CompilerParams(vmem_limit_bytes=VMEM_LIMIT),
        cost_estimate=pl.CostEstimate(flops=2 * 512 * 1280 * 64, bytes_accessed=3 << 20, transcendentals=0),
    )(where, dq, dk, dv, pq, pk, pv)


def sketch_kernel(hidden, gain, proj, out):
    rows = hidden[...].astype(F32)
    inv = lax.rsqrt(jnp.mean(rows * rows, axis=1, keepdims=True) + EPSILON)
    normed = (rows * inv * gain[...]).astype(BF)
    out[...] = jnp.dot(normed, proj[...], preferred_element_type=F32).astype(BF)


def sketch(hidden, gain, proj):
    return pl.pallas_call(
        sketch_kernel,
        out_shape=jax.ShapeDtypeStruct((TOK, 64), BF),
        compiler_params=pltpu.CompilerParams(vmem_limit_bytes=VMEM_LIMIT),
        cost_estimate=pl.CostEstimate(flops=2 * 64 * 8192 * 64, bytes_accessed=4 << 20, transcendentals=0),
    )(hidden, gain, proj)


FEATURES = [(r, s) for r in (0, 1, 3, 2) for s in (0, 1)]


def finish_kernel(pos, hidden, gain, q0, q1, q2, q3, out):
    x, z, c = pos[0], pos[1], pos[2]
    rows = hidden[...].astype(F32)
    inv = lax.rsqrt(jnp.mean(rows * rows, axis=1, keepdims=True) + EPSILON)

    def blocks():
        for j, q in enumerate((q0, q1, q2, q3)):
            for b, (r, s) in enumerate(FEATURES):
                block = lax.rem(x + 4 - j, 4) * 8 + lax.rem(z + r, 4) * 2 + (c + s) % 2
                cols = pl.ds(pl.multiple_of(block * 256, 256), 256)
                grad = q[:, b * 256 : b * 256 + 256].astype(F32) * gain[:, cols]
                yield cols, grad, hidden[:, cols].astype(F32) * inv

    total = jnp.zeros((TOK, 256), F32)
    for cols, grad, unit in blocks():
        total += grad * unit
    mean = jnp.sum(total, axis=1, keepdims=True) * (1.0 / 8192)
    for cols, grad, unit in blocks():
        out[:, cols] = (inv * (grad - unit * mean)).astype(BF)


def finish(pos, hidden, gain, parts):
    vmem = pl.BlockSpec(memory_space=pltpu.VMEM)
    return pl.pallas_call(
        finish_kernel,
        in_specs=[pl.BlockSpec(memory_space=pltpu.SMEM)] + [vmem] * 6,
        out_specs=vmem,
        out_shape=jax.ShapeDtypeStruct((TOK, 8192), BF),
        compiler_params=pltpu.CompilerParams(vmem_limit_bytes=VMEM_LIMIT),
        cost_estimate=pl.CostEstimate(flops=10 * 64 * 8192, bytes_accessed=4 << 20, transcendentals=0),
    )(pos, hidden, gain, *parts)


def times_weights(cot, weights):
    return lax.dot_general(
        cot, weights, (((1,), (1,)), ((), ())), preferred_element_type=F32
    ).astype(BF)


def add(*terms):
    total = terms[0].astype(F32)
    for term in terms[1:]:
        total = total + term.astype(F32)
    return total.astype(BF)


def sum_over_tensor(cots, weights):
    n = len(cots)
    part = {}
    for k in (2, 1, 3, 0):
        rows = jnp.concatenate([cot[k * 128 : k * 128 + 128] for cot in cots], axis=0)
        part[k] = times_weights(rows, weights)
    half = part[0].shape[1] // 2
    far_up = along_y(part[2][:, :half], 1)
    far_down = along_y(part[2][:, half:], -1)
    near_up = along_y(part[1][:, half:], 1)
    near_down = along_y(part[3][:, :half], -1)
    rest_up = along_y(add(part[1][:, :half], far_up), 1)
    rest_down = along_y(add(part[3][:, half:], far_down), -1)
    total = jnp.concatenate(
        [
            add(part[0][:, :half], near_down, rest_up),
            add(part[0][:, half:], near_up, rest_down),
        ],
        axis=1,
    ).reshape(n, 2, TOK, 2 * half)
    got = swap_l(total[:, 1])
    return add(total[:, 0], got)


def local(
    hidden,
    norm_gain,
    w_query,
    w_key,
    w_value,
    d_query,
    d_key,
    d_value,
    lengths,
    proj_in,
    proj_query,
    proj_key,
    proj_value,
    queries,
):
    dp, tensor = lax.axis_index("dp"), lax.axis_index("tensor")
    x, z, c, y, low = dp // 8, dp // 2 % 4, dp % 2, tensor // 2, tensor % 2
    gain = norm_gain.reshape(1, -1)

    where = jnp.stack([(y + k) % 4 * 2 + (low + l) % 2 for k in range(4) for l in range(2)])
    cot, head = prepare(
        where.astype(jnp.int32), d_query, d_key, d_value, proj_query, proj_key, proj_value
    )
    w0 = jnp.concatenate([w_query, w_key, w_value], axis=1)

    d1, d3 = along_x(cot, -1), along_x(cot, 1)
    w1, w3 = along_z(w0, -1), along_z(w0, 1)
    o0 = other_core(w0)
    d2 = jnp.concatenate([along_x(d1[:256], -1), along_x(d3[256:], 1)], axis=0)
    w2 = jnp.concatenate([along_z(w1[:128], -1), along_z(w3[128:], 1)], axis=0)
    o1, o3, o2 = other_core(w1), other_core(w3), other_core(w2)
    weights = jnp.concatenate([w0, o0, w1, o1, w3, o3, w2, o2], axis=0)

    tokens = sketch(hidden, gain, proj_in)
    head = head.reshape(4, 128, 192)
    head = add(head[0], along_y(head[1], 1), along_y(head[3], -1), along_y(head[2], 2))
    head = head.reshape(2, TOK, 192)
    head = head[0].astype(F32) + swap_l(head[1]).astype(F32)
    at = tensor % 4 * TOK + lax.broadcasted_iota(jnp.int32, (TOK, 1), 0)
    head = jnp.where(at < lengths[tensor // 4], head, 0.0)
    own = lax.dot_general(
        tokens.astype(F32), head, (((0,), (0,)), ((), ())), precision=lax.Precision.HIGHEST
    )
    own = own.reshape(64, 3, 64).transpose(1, 0, 2).reshape(96, 128)
    own = own + swap_l(own)
    pair = own + swap_y(own, 1)
    rest = swap_y(pair, 2)
    grads = jnp.stack(
        [jnp.where(y < 2, pair, rest), jnp.where(y < 2, rest, pair)]
    ).astype(BF)
    grads = jnp.stack([grads, along_z(grads, -1), along_z(grads, 2), along_z(grads, 1)])
    grads = jnp.stack([grads, along_x(grads, -1), along_x(grads, 2), along_x(grads, 1)])
    grads = jnp.stack([grads, other_core(grads)])
    grads = grads.reshape(64, 12288)
    scores = lax.dot_general(grads, queries, (((1,), (1,)), ((), ())), preferred_element_type=F32)
    row = jnp.arange(64)
    rx, rz, rc, ru = row // 16, row // 4 % 4, row // 2 % 2, row % 2
    source = (rc + c) % 2 * 32 + (rx + 4 - x) % 4 * 8 + (rz + 4 - z) % 4 * 2 + ru
    scores = jnp.take(scores, source, axis=0)

    first = sum_over_tensor([d2, d1], weights)
    second = sum_over_tensor([d3, cot], weights)
    parts = [
        second[1],
        along_x(first[1], 1),
        along_x(first[0], 2),
        along_x(second[0], -1),
    ]
    pos = jnp.stack([x, z, c]).astype(jnp.int32)
    return scores, finish(pos, hidden, gain, parts)


def solution(mesh):
    placed = (
        P(("dp", "tensor"), None),
        P(),
        P("dp", "tensor"),
        P("dp", "tensor"),
        P("dp", "tensor"),
        P("dp", "tensor"),
        P("dp", "tensor"),
        P("dp", "tensor"),
        P("dp"),
        P(),
        P("tensor", None),
        P("tensor", None),
        P("tensor", None),
        P(("dp", "tensor"), None),
    )
    return jax.shard_map(
        local,
        mesh=mesh,
        in_specs=placed,
        out_specs=(P(None, ("dp", "tensor")), P(("dp", "tensor"), None)),
        check_vma=False,
    )
```

```python
import functools

import jax
import jax.numpy as jnp
from jax import lax
from jax.experimental import pallas as pl
from jax.experimental.pallas import tpu as pltpu
from jax.sharding import PartitionSpec as P

EPSILON = 1e-05
BF = jnp.bfloat16
F32 = jnp.float32
VMEM_LIMIT = 48 * 1024 * 1024

NX, NZ, NC, NY, NL = 4, 4, 2, 4, 2
TOK = 64


def along_x(v, step):
    return lax.ppermute(v, "dp", [(i, (i // 8 + step) % NX * 8 + i % 8) for i in range(32)])


def along_z(v, step):
    return lax.ppermute(
        v, "dp", [(i, i // 8 * 8 + (i // 2 + step) % NZ * 2 + i % 2) for i in range(32)]
    )


def other_core(v):
    return lax.ppermute(v, "dp", [(i, i ^ 1) for i in range(32)])


def along_y(v, step):
    return lax.ppermute(v, "tensor", [(t, (t // 2 + step) % NY * 2 + t % 2) for t in range(8)])


def swap_l(v):
    return lax.ppermute(v, "tensor", [(t, t ^ 1) for t in range(8)])


def prepare_kernel(where, dq, dk, dv, cot):
    cot[:, :1024] = dq[...]
    cot[:, 1024:1152] = dk[...]
    cot[:, 1152:] = dv[...]


def prepare(where, dq, dk, dv):
    rows = lambda b, where: (where[b], 0)
    return pl.pallas_call(
        prepare_kernel,
        grid_spec=pltpu.PrefetchScalarGridSpec(
            num_scalar_prefetch=1,
            grid=(8,),
            in_specs=[
                pl.BlockSpec((TOK, 1024), rows),
                pl.BlockSpec((TOK, 128), rows),
                pl.BlockSpec((TOK, 128), rows),
            ],
            out_specs=pl.BlockSpec((TOK, 1280), lambda b, where: (b, 0)),
        ),
        out_shape=jax.ShapeDtypeStruct((512, 1280), BF),
        compiler_params=pltpu.CompilerParams(vmem_limit_bytes=VMEM_LIMIT),
        cost_estimate=pl.CostEstimate(flops=1, bytes_accessed=1, transcendentals=0),
    )(where, dq, dk, dv)


def side_by_side_kernel(q, k, v, out, sems):
    copies = []
    for ref, col in ((q, 0), (k, 1024), (v, 1152)):
        to = out.at[:, col : col + ref.shape[1]]
        copies.append(pltpu.make_async_copy(ref, to, sems.at[len(copies)]))
    for copy in copies:
        copy.start()
    for copy in copies:
        copy.wait()


def copied(kernel, rows, args, copies, scalars=()):
    hbm = pl.BlockSpec(memory_space=pltpu.HBM)
    return pl.pallas_call(
        kernel,
        in_specs=[pl.BlockSpec(memory_space=pltpu.SMEM)] * len(scalars) + [hbm] * len(args),
        out_specs=hbm,
        out_shape=shape(rows, 1280),
        scratch_shapes=[pltpu.SemaphoreType.DMA((copies,))],
        compiler_params=pltpu.CompilerParams(vmem_limit_bytes=VMEM_LIMIT),
        cost_estimate=pl.CostEstimate(flops=1, bytes_accessed=1, transcendentals=0),
    )(*scalars, *args)


def call(kernel, shapes, args, scratch=(), scalars=()):
    vmem = pl.BlockSpec(memory_space=pltpu.VMEM)
    return pl.pallas_call(
        kernel,
        in_specs=[pl.BlockSpec(memory_space=pltpu.SMEM)] * len(scalars) + [vmem] * len(args),
        out_specs=[vmem] * len(shapes),
        out_shape=list(shapes),
        scratch_shapes=list(scratch),
        compiler_params=pltpu.CompilerParams(vmem_limit_bytes=VMEM_LIMIT),
        cost_estimate=pl.CostEstimate(flops=1, bytes_accessed=1, transcendentals=0),
    )(*scalars, *args)


def shape(*dims):
    return jax.ShapeDtypeStruct(dims, BF)


def dot_t(left, right):
    return lax.dot_general(left, right, (((1,), (1,)), ((), ())), preferred_element_type=F32)


def head_kernel(where, d, pq, pk, pv, head):
    for m, (p, lo, hi) in enumerate(((pq, 0, 1024), (pk, 1024, 1152), (pv, 1152, 1280))):
        found = dot_t(d[:, lo:hi], p[...]).astype(BF)
        for b in range(8):
            rows = pl.ds(pl.multiple_of(where[b] * TOK, TOK), TOK)
            head[rows, m * 64 : m * 64 + 64] = found[b * TOK : b * TOK + TOK]


def sketch_kernel(hidden, gain, proj, out):
    rows = hidden[...].astype(F32)
    inv = lax.rsqrt(jnp.mean(rows * rows, axis=1, keepdims=True) + EPSILON)
    normed = (rows * inv * gain[...]).astype(BF)
    out[...] = dot_t(normed, proj[...]).astype(BF)


def outer_kernel(live, tokens, heads, out):
    head = heads[0:128].astype(F32)
    for t in range(1, 4):
        head = head + heads[t * 128 : t * 128 + 128].astype(F32)
    at = lax.broadcasted_iota(jnp.int32, (128, 192), 0)
    head = jnp.where(at < live[0], head, 0.0)
    to = lax.broadcasted_iota(jnp.int32, (64, 64), 1)
    source = jnp.where(to < 32, 2 * to, 2 * to - 63)
    pick = (lax.broadcasted_iota(jnp.int32, (64, 64), 0) == source).astype(F32).astype(BF)
    ordered = jnp.dot(tokens[...], pick, preferred_element_type=F32)
    for m in range(3):
        part = lax.dot_general(
            ordered,
            head[:, m * 64 : m * 64 + 64],
            (((0,), (0,)), ((), ())),
            precision=lax.Precision.HIGHEST,
            preferred_element_type=F32,
        ).astype(BF)
        for t in range(4):
            out[t, m * 32 : m * 32 + 32, :64] = part[:32]
            out[t, m * 32 : m * 32 + 32, 64:] = part[32:]


STAGE1 = [(j, r) for j in (0, 1, 3) for r in (0, 1, 3)]
STAGE2 = [(2, r) for r in (0, 1, 3, 2)] + [(j, 2) for j in (0, 1, 3)]
COLS1, COLS2 = 256 * len(STAGE1), 256 * len(STAGE2)


def product(blocks, js, rs, hs, ks, ds, ws, outs, left):
    n = 0
    for j in js:
        for k in ks:
            left[n * 128 : n * 128 + 128] = ds[j][k * 128 : k * 128 + 128]
            n += 1
    for h in hs:
        for r in rs:
            found = dot_t(left[: n * 128], ws[r][h][...]).astype(BF)
            m = 0
            for j in js:
                col = blocks.index((j, r)) * 256
                for k in ks:
                    outs[k][h][:, col : col + 256] = found[m * 128 : m * 128 + 128]
                    m += 1


def far1_kernel(h, d0, d1, d3, w0, w1, w3, out, left):
    ws = {r: {h: w} for r, w in ((0, w0), (1, w1), (3, w3))}
    product(STAGE1, (0, 1, 3), (0, 1, 3), (h,), (2,), {0: d0, 1: d1, 3: d3}, ws, {2: {h: out}}, left)


def near1_kernel(d0, d1, d3, w0, o0, w1, o1, w3, o3, one, three, own, left):
    ws = {0: (w0, o0), 1: (w1, o1), 3: (w3, o3)}
    outs = {k: (out.at[0], out.at[1]) for k, out in ((1, one), (3, three), (0, own))}
    product(STAGE1, (0, 1, 3), (0, 1, 3), (0, 1), (1, 3, 0), {0: d0, 1: d1, 3: d3}, ws, outs, left)


def stage2_kernel(d0, d1, d3, d2, w0, o0, w1, o1, w3, o3, w2, o2, far0, far1, one, three, own, left):
    ds = {0: d0, 1: d1, 3: d3, 2: d2}
    ws = {0: (w0, o0), 1: (w1, o1), 3: (w3, o3), 2: (w2, o2)}
    outs = {k: (out.at[0], out.at[1]) for k, out in ((1, one), (3, three), (0, own))}
    outs[2] = (far0, far1)
    product(STAGE2, (2,), (0, 1, 3, 2), (0, 1), (2, 1, 3, 0), ds, ws, outs, left)
    product(STAGE2, (0, 1, 3), (2,), (0, 1), (2, 1, 3, 0), ds, ws, outs, left)


def finish_kernel(pos, hidden, gain, e0, e1, e3, f0, f1, f3, f2, out):
    x, z, c = pos[0], pos[1], pos[2]
    rows = hidden[...].astype(F32)
    inv = lax.rsqrt(jnp.mean(rows * rows, axis=1, keepdims=True) + EPSILON)
    places = {(2, r): (f2, i * 256) for i, r in enumerate((0, 1, 3, 2))}
    for j, first, second in ((0, e0, f0), (1, e1, f1), (3, e3, f3)):
        places.update({(j, r): (first, i * 256) for i, r in enumerate((0, 1, 3))})
        places[j, 2] = (second, 0)

    def blocks():
        for (j, r), (ref, col) in places.items():
            for h in range(2):
                block = lax.rem(x + 4 - j, 4) * 8 + lax.rem(z + r, 4) * 2 + lax.rem(c + h, 2)
                cols = pl.ds(pl.multiple_of(block * 256, 256), 256)
                grad = ref[h, :, col : col + 256].astype(F32) * gain[:, cols]
                yield cols, grad, hidden[:, cols].astype(F32) * inv

    total = jnp.zeros((TOK, 256), F32)
    for cols, grad, unit in blocks():
        total += grad * unit
    mean = jnp.sum(total, axis=1, keepdims=True) * (1.0 / 8192)
    for cols, grad, unit in blocks():
        out[:, cols] = (inv * (grad - unit * mean)).astype(BF)


def add(*terms):
    total = terms[0].astype(F32)
    for term in terms[1:]:
        total = total + term.astype(F32)
    return total.astype(BF)


def second_kernel(far_up, far_down, one, three, up, down):
    up[0] = add(one[0], far_up[...])
    up[1] = one[1]
    down[0] = three[0]
    down[1] = add(three[1], far_down[...])


def second2_kernel(far_up, far_down, one, three, up2, down2, up3, down3):
    for up, down, lo, hi in ((up2, down2, 0, 1024), (up3, down3, 1024, 1792)):
        up[0] = add(one[0, :, lo:hi], far_up[:, lo:hi])
        up[1] = one[1, :, lo:hi]
        down[0] = three[0, :, lo:hi]
        down[1] = add(three[1, :, lo:hi], far_down[:, lo:hi])


def third_kernel(own, up, down, keep, send, col=0):
    cols = slice(col, col + up.shape[2])
    keep[...] = add(own[:, :TOK, cols], up[:, :TOK], down[:, :TOK])
    send[...] = add(own[:, TOK:, cols], up[:, TOK:], down[:, TOK:])


def split_kernel(keep, got, *outs):
    col = 0
    for out in outs:
        end = col + out.shape[2]
        out[...] = add(keep[:, :, col:end], got[:, :, col:end])
        col = end


def to_all(v, groups):
    copies = jnp.broadcast_to(v[None], (len(groups[0]), *v.shape))
    v = lax.all_to_all(copies, "dp", 0, 0, axis_index_groups=groups)
    return v.reshape(-1, 96, 128)


def local(
    hidden,
    norm_gain,
    w_query,
    w_key,
    w_value,
    d_query,
    d_key,
    d_value,
    lengths,
    proj_in,
    proj_query,
    proj_key,
    proj_value,
    queries,
):
    dp, tensor = lax.axis_index("dp"), lax.axis_index("tensor")
    x, z, c, y, low = dp // 8, dp // 2 % 4, dp % 2, tensor // 2, tensor % 2
    gain = norm_gain.reshape(1, -1)

    (tokens,) = call(sketch_kernel, [shape(TOK, 64)], [hidden, gain, proj_in.T])
    d_query, w_query, tokens = lax.optimization_barrier((d_query, w_query, tokens))
    other = swap_l(tokens)

    where = jnp.stack([(y + k) % 4 * 2 + (low + l) % 2 for k in range(4) for l in range(2)])
    where = where.astype(jnp.int32)
    d0 = prepare(where, d_query, d_key, d_value)
    d1, d3 = along_x(d0, -1), along_x(d0, 1)
    w0 = copied(side_by_side_kernel, 256, [w_query, w_key, w_value], 3)
    w0, other = lax.optimization_barrier((w0, other))
    tokens = jnp.concatenate([jnp.where(low == 0, tokens, other), jnp.where(low == 0, other, tokens)])

    w1, w3 = along_z(w0, -1), along_z(w0, 1)
    o0 = other_core(w0)

    (head,) = call(
        head_kernel,
        [shape(512, 192)],
        [d0, proj_query.T, proj_key.T, proj_value.T],
        scalars=[where],
    )
    over_y = dict(axis_index_groups=[[0, 2, 4, 6], [1, 3, 5, 7]], tiled=True)
    heads = lax.all_to_all(head, "tensor", 0, 0, **over_y)
    live = (lengths[y // 2] - y % 2 * 128).reshape(1)
    (outer,) = call(outer_kernel, [shape(4, 96, 128)], [tokens, heads], scalars=[live])
    outer = lax.all_to_all(outer, "tensor", 0, 0, **over_y)
    grads = jnp.sum(outer.reshape(2, 2, 96, 128).astype(F32), axis=1)

    d0, w0, o0, d1, d3, w1, w3, grads = lax.optimization_barrier((d0, w0, o0, d1, d3, w1, w3, grads))
    d2, w2 = along_x(d0, 2), along_z(w0, 2)
    grads = (grads + swap_l(grads)).astype(BF)
    o1, o3 = other_core(w1), other_core(w3)

    far0, far1 = (
        call(
            functools.partial(far1_kernel, h),
            [shape(128, COLS1)],
            [d0, d1, d3, *ws],
            [pltpu.VMEM((384, 1280), BF)],
        )[0]
        for h, ws in enumerate(((w0, w1, w3), (o0, o1, o3)))
    )
    grads, _ = lax.optimization_barrier((grads, far1))
    grads = to_all(grads, [[x * 8 + i for i in range(8)] for x in range(4)])
    far0, far1 = along_y(far0, 1), along_y(far1, -1)
    one, three, own = call(
        near1_kernel,
        [shape(2, 128, COLS1)] * 3,
        [d0, d1, d3, w0, o0, w1, o1, w3, o3],
        [pltpu.VMEM((1152, 1280), BF)],
    )
    steps = shape(2, 128, COLS1)
    up, down = call(second_kernel, [steps] * 2, [far0, far1, one, three])
    d2, w2, _, _ = lax.optimization_barrier((d2, w2, up, down))
    up, down = along_y(up, 1), along_y(down, -1)

    o2 = other_core(w2)
    steps = shape(2, 128, COLS2)
    far0, far1, one2, three2, own2 = call(
        stage2_kernel,
        [shape(128, COLS2)] * 2 + [steps] * 3,
        [d0, d1, d3, d2, w0, o0, w1, o1, w3, o3, w2, o2],
        [pltpu.VMEM((1536, 1280), BF)],
    )
    grads, _ = lax.optimization_barrier((grads, far1))
    grads = to_all(grads, [[x * 8 + i for x in range(4)] for i in range(8)])
    far0, far1 = along_y(far0, 1), along_y(far1, -1)

    up, down, far0, far1 = lax.optimization_barrier((up, down, far0, far1))
    mid, low_cols = shape(2, 128, 1024), shape(2, 128, 768)
    up2, down2, up3, down3 = call(
        second2_kernel, [mid, mid, low_cols, low_cols], [far0, far1, one2, three2]
    )
    up2, down2 = along_y(up2, 1), along_y(down2, -1)
    up3, down3 = along_y(up3, 1), along_y(down3, -1)
    keep, send = call(third_kernel, [shape(2, TOK, COLS1)] * 2, [own, up, down])
    got = swap_l(send)
    e0, e1, e3 = call(split_kernel, [shape(2, TOK, 768)] * 3, [keep, got])
    e1, e3 = along_x(e1, 1), along_x(e3, -1)
    keep, send = call(third_kernel, [shape(2, TOK, 1024)] * 2, [own2, up2, down2])
    (f2,) = call(split_kernel, [shape(2, TOK, 1024)], [keep, swap_l(send)])
    f2 = along_x(f2, 2)
    up3, down3, _, _ = lax.optimization_barrier((up3, down3, up2, down2))
    keep, send = call(
        functools.partial(third_kernel, col=1024), [shape(2, TOK, 768)] * 2, [own2, up3, down3]
    )
    f0, f1, f3 = call(split_kernel, [shape(2, TOK, 256)] * 3, [keep, swap_l(send)])
    f1, f3 = along_x(f1, 1), along_x(f3, -1)
    scores = dot_t(grads.reshape(64, 12288), queries)

    pos = jnp.stack([x, z, c]).astype(jnp.int32)
    (grad_hidden,) = call(
        finish_kernel,
        [shape(TOK, 8192)],
        [hidden, gain, e0, e1, e3, f0, f1, f3, f2],
        scalars=[pos],
    )
    return scores, grad_hidden


def solution(mesh):
    placed = (
        P(("dp", "tensor"), None),
        P(),
        P("dp", "tensor"),
        P("dp", "tensor"),
        P("dp", "tensor"),
        P("dp", "tensor"),
        P("dp", "tensor"),
        P("dp", "tensor"),
        P("dp"),
        P(),
        P("tensor", None),
        P("tensor", None),
        P("tensor", None),
        P(("dp", "tensor"), None),
    )
    return jax.shard_map(
        local,
        mesh=mesh,
        in_specs=placed,
        out_specs=(P(None, ("dp", "tensor")), P(("dp", "tensor"), None)),
        check_vma=False,
    )
```

```python
import functools

import jax
import jax.numpy as jnp
from jax import lax
from jax.experimental import pallas as pl
from jax.experimental.pallas import tpu as pltpu
from jax.sharding import PartitionSpec as P

EPSILON = 1e-05
BF = jnp.bfloat16
F32 = jnp.float32
VMEM_LIMIT = 48 * 1024 * 1024
VMEM_ALL = 60 * 1024 * 1024

NX, NZ, NC, NY, NL = 4, 4, 2, 4, 2
TOK = 64


def along_x(v, step):
    return lax.ppermute(v, "dp", [(i, (i // 8 + step) % NX * 8 + i % 8) for i in range(32)])


def along_z(v, step):
    return lax.ppermute(
        v, "dp", [(i, i // 8 * 8 + (i // 2 + step) % NZ * 2 + i % 2) for i in range(32)]
    )


def other_core(v):
    return lax.ppermute(v, "dp", [(i, i ^ 1) for i in range(32)])


def along_y(v, step):
    return lax.ppermute(v, "tensor", [(t, (t // 2 + step) % NY * 2 + t % 2) for t in range(8)])


def swap_l(v):
    return lax.ppermute(v, "tensor", [(t, t ^ 1) for t in range(8)])


def prepare_kernel(place, dq, dk, dv, out, held, came, went):
    arrivals, departures = [], []
    for b in range(8):
        low = lax.rem(place[1] + b % 2, 2)
        rows = pl.ds(pl.multiple_of((place[0] + b // 2) % 4 * 128 + low * TOK, TOK), TOK)
        to = slice(b * TOK, b * TOK + TOK)
        for i, (ref, col) in enumerate(((dq, 0), (dk, 1024), (dv, 1152))):
            part = held.at[to, col : col + ref.shape[1]]
            arrivals.append(pltpu.make_async_copy(ref.at[rows], part, came.at[3 * b + i]))
        departures.append(pltpu.make_async_copy(held.at[to], out.at[to], went.at[b]))
    send_on(arrivals, departures)


def side_by_side_kernel(q, k, v, out, held, came, went):
    arrivals, departures = [], []
    for b in range(4):
        rows = slice(b * 64, b * 64 + 64)
        for i, (ref, col) in enumerate(((q, 0), (k, 1024), (v, 1152))):
            part = held.at[rows, col : col + ref.shape[1]]
            arrivals.append(pltpu.make_async_copy(ref.at[rows], part, came.at[3 * b + i]))
        departures.append(pltpu.make_async_copy(held.at[rows], out.at[rows], went.at[b]))
    send_on(arrivals, departures)


def send_on(arrivals, departures):
    for copy in arrivals:
        copy.start()
    for b, copy in enumerate(departures):
        for arrival in arrivals[3 * b : 3 * b + 3]:
            arrival.wait()
        copy.start()
    for copy in departures:
        copy.wait()


def copied(kernel, rows, blocks, args, scalars=()):
    hbm = pl.BlockSpec(memory_space=pltpu.HBM)
    return pl.pallas_call(
        kernel,
        in_specs=[pl.BlockSpec(memory_space=pltpu.SMEM)] * len(scalars) + [hbm] * len(args),
        out_specs=hbm,
        out_shape=shape(rows, 1280),
        scratch_shapes=[
            pltpu.VMEM((rows, 1280), BF),
            pltpu.SemaphoreType.DMA((3 * blocks,)),
            pltpu.SemaphoreType.DMA((blocks,)),
        ],
        compiler_params=pltpu.CompilerParams(vmem_limit_bytes=VMEM_ALL),
        cost_estimate=pl.CostEstimate(flops=1, bytes_accessed=1, transcendentals=0),
    )(*scalars, *args)


def call(kernel, shapes, args, scratch=(), scalars=(), vmem_limit=VMEM_LIMIT, flops=1):
    vmem = pl.BlockSpec(memory_space=pltpu.VMEM)
    return pl.pallas_call(
        kernel,
        in_specs=[pl.BlockSpec(memory_space=pltpu.SMEM)] * len(scalars) + [vmem] * len(args),
        out_specs=[vmem] * len(shapes),
        out_shape=list(shapes),
        scratch_shapes=list(scratch),
        compiler_params=pltpu.CompilerParams(vmem_limit_bytes=vmem_limit),
        cost_estimate=pl.CostEstimate(flops=flops, bytes_accessed=1, transcendentals=0),
    )(*scalars, *args)


def shape(*dims):
    return jax.ShapeDtypeStruct(dims, BF)


def dot_t(left, right):
    return lax.dot_general(left, right, (((1,), (1,)), ((), ())), preferred_element_type=F32)


def head_kernel(place, d, pq, pk, pv, head):
    for m, (p, lo, hi) in enumerate(((pq, 0, 1024), (pk, 1024, 1152), (pv, 1152, 1280))):
        found = dot_t(d[:, lo:hi], p[...]).astype(BF)
        for b in range(8):
            to = (place[0] + b // 2) % 4 * 128 + (place[1] + b % 2) % 2 * TOK
            head[pl.ds(pl.multiple_of(to, TOK), TOK), m * 64 : m * 64 + 64] = found[
                b * TOK : b * TOK + TOK
            ]


def sketch_kernel(hidden, gain, proj, out):
    rows = hidden[...].astype(F32)
    inv = lax.rsqrt(jnp.mean(rows * rows, axis=1, keepdims=True) + EPSILON)
    normed = (rows * inv * gain[...]).astype(BF)
    out[...] = dot_t(normed, proj[...]).astype(BF)


def outer_kernel(live, tokens, heads, out):
    head = heads[0:128].astype(F32)
    for t in range(1, 4):
        head = head + heads[t * 128 : t * 128 + 128].astype(F32)
    at = lax.broadcasted_iota(jnp.int32, (128, 192), 0)
    head = jnp.where(at < live[0], head, 0.0)
    to = lax.broadcasted_iota(jnp.int32, (64, 64), 1)
    source = jnp.where(to < 32, 2 * to, 2 * to - 63)
    pick = (lax.broadcasted_iota(jnp.int32, (64, 64), 0) == source).astype(F32).astype(BF)
    ordered = jnp.dot(tokens[...], pick, preferred_element_type=F32)
    for m in range(3):
        part = lax.dot_general(
            ordered,
            head[:, m * 64 : m * 64 + 64],
            (((0,), (0,)), ((), ())),
            precision=lax.Precision.HIGHEST,
            preferred_element_type=F32,
        ).astype(BF)
        for t in range(4):
            out[t, m * 32 : m * 32 + 32, :64] = part[:32]
            out[t, m * 32 : m * 32 + 32, 64:] = part[32:]


STAGE1 = [(j, r) for j in (0, 1, 3) for r in (0, 1, 3)]
STAGE2 = [(2, r) for r in (0, 1, 3, 2)] + [(j, 2) for j in (0, 1, 3)]
COLS1, COLS2 = 256 * len(STAGE1), 256 * len(STAGE2)


def product(blocks, js, rs, hs, ks, ds, ws, outs, left):
    n = 0
    for j in js:
        for k in ks:
            left[n * 128 : n * 128 + 128] = ds[j][k * 128 : k * 128 + 128]
            n += 1
    for h in hs:
        for r in rs:
            found = dot_t(left[: n * 128], ws[r][h][...]).astype(BF)
            m = 0
            for j in js:
                col = blocks.index((j, r)) * 256
                for k in ks:
                    outs[k][h][:, col : col + 256] = found[m * 128 : m * 128 + 128]
                    m += 1


def far1_kernel(d0, d1, d3, w0, w1, w3, out, left):
    for n, ref in enumerate((d0, d1, d3)):
        left[n * 128 : n * 128 + 128] = ref[...]
    for i, w in enumerate((w0, w1, w3)):
        found = dot_t(left[...], w[...]).astype(BF)
        for n in range(3):
            col = (3 * n + i) * 256
            out[:, col : col + 256] = found[n * 128 : n * 128 + 128]


def far1_terms(ds, ws):
    return pl.pallas_call(
        far1_kernel,
        grid=(1,),
        in_specs=[pl.BlockSpec((128, 1280), lambda i: (2, 0))] * 3
        + [pl.BlockSpec((256, 1280), lambda i: (0, 0))] * 3,
        out_specs=pl.BlockSpec((128, COLS1), lambda i: (0, 0)),
        out_shape=shape(128, COLS1),
        scratch_shapes=[pltpu.VMEM((384, 1280), BF)],
        compiler_params=pltpu.CompilerParams(vmem_limit_bytes=VMEM_ALL),
        cost_estimate=pl.CostEstimate(flops=1, bytes_accessed=1, transcendentals=0),
    )(*ds, *ws)


def near1_kernel(d0, d1, d3, w0, o0, w1, o1, w3, o3, one, three, own, left):
    ws = {0: (w0, o0), 1: (w1, o1), 3: (w3, o3)}
    outs = {k: (out.at[0], out.at[1]) for k, out in ((1, one), (3, three), (0, own))}
    product(STAGE1, (0, 1, 3), (0, 1, 3), (0, 1), (1, 3, 0), {0: d0, 1: d1, 3: d3}, ws, outs, left)


def stage2_kernel(d0, d1, d3, d2, w0, o0, w1, o1, w3, o3, w2, o2, far0, far1, one, three, own, left):
    ds = {0: d0, 1: d1, 3: d3, 2: d2}
    ws = {0: (w0, o0), 1: (w1, o1), 3: (w3, o3), 2: (w2, o2)}
    outs = {k: (out.at[0], out.at[1]) for k, out in ((1, one), (3, three), (0, own))}
    outs[2] = (far0, far1)
    product(STAGE2, (2,), (0, 1, 3, 2), (0, 1), (2, 1, 3, 0), ds, ws, outs, left)
    product(STAGE2, (0, 1, 3), (2,), (0, 1), (2, 1, 3, 0), ds, ws, outs, left)


def finish_kernel(place, hidden, gain, e0, e1, e3, f0, f1, f3, f2, out):
    x, z, c = place[2], place[3], place[4]
    rows = hidden[...].astype(F32)
    inv = lax.rsqrt(jnp.mean(rows * rows, axis=1, keepdims=True) + EPSILON)
    places = {(2, r): (f2, i * 256) for i, r in enumerate((0, 1, 3, 2))}
    for j, first, second in ((0, e0, f0), (1, e1, f1), (3, e3, f3)):
        places.update({(j, r): (first, i * 256) for i, r in enumerate((0, 1, 3))})
        places[j, 2] = (second, 0)

    def blocks():
        for (j, r), (ref, col) in places.items():
            for h in range(2):
                block = lax.rem(x + 4 - j, 4) * 8 + lax.rem(z + r, 4) * 2 + lax.rem(c + h, 2)
                cols = pl.ds(pl.multiple_of(block * 256, 256), 256)
                grad = ref[h, :, col : col + 256].astype(F32) * gain[:, cols]
                yield cols, grad, hidden[:, cols].astype(F32) * inv

    total = jnp.zeros((TOK, 256), F32)
    for cols, grad, unit in blocks():
        total += grad * unit
    mean = jnp.sum(total, axis=1, keepdims=True) * (1.0 / 8192)
    for cols, grad, unit in blocks():
        out[:, cols] = (inv * (grad - unit * mean)).astype(BF)


def add(*terms):
    total = terms[0].astype(F32)
    for term in terms[1:]:
        total = total + term.astype(F32)
    return total.astype(BF)


def second_kernel(far_up, far_down, one, three, up, down):
    up[0] = add(one[0], far_up[...])
    up[1] = one[1]
    down[0] = three[0]
    down[1] = add(three[1], far_down[...])


def second2_kernel(far_up, far_down, one, three, up2, down2, up3, down3):
    for up, down, lo, hi in ((up2, down2, 0, 1024), (up3, down3, 1024, 1792)):
        up[0] = add(one[0, :, lo:hi], far_up[:, lo:hi])
        up[1] = one[1, :, lo:hi]
        down[0] = three[0, :, lo:hi]
        down[1] = add(three[1, :, lo:hi], far_down[:, lo:hi])


def third_kernel(own, up, down, keep, send, col=0):
    cols = slice(col, col + up.shape[2])
    keep[...] = add(own[:, :TOK, cols], up[:, :TOK], down[:, :TOK])
    send[...] = add(own[:, TOK:, cols], up[:, TOK:], down[:, TOK:])


def split_kernel(keep, got, *outs):
    col = 0
    for out in outs:
        end = col + out.shape[2]
        out[...] = add(keep[:, :, col:end], got[:, :, col:end])
        col = end


def to_all(v, groups):
    copies = jnp.broadcast_to(v[None], (len(groups[0]), *v.shape))
    v = lax.all_to_all(copies, "dp", 0, 0, axis_index_groups=groups)
    return v.reshape(-1, 96, 128)


def local(
    hidden,
    norm_gain,
    w_query,
    w_key,
    w_value,
    d_query,
    d_key,
    d_value,
    lengths,
    proj_in,
    proj_query,
    proj_key,
    proj_value,
    queries,
):
    dp, tensor = lax.axis_index("dp"), lax.axis_index("tensor")
    x, z, c, y, low = dp // 8, dp // 2 % 4, dp % 2, tensor // 2, tensor % 2
    gain = norm_gain.reshape(1, -1)

    (tokens,) = call(
        sketch_kernel, [shape(TOK, 64)], [hidden, gain, proj_in.T], vmem_limit=VMEM_ALL
    )
    other = swap_l(tokens)

    place = jnp.stack([y, low, x, z, c]).astype(jnp.int32)
    w0 = copied(side_by_side_kernel, 256, 4, [w_query, w_key, w_value])
    w0, other = lax.optimization_barrier((w0, other))
    tokens = jnp.concatenate([jnp.where(low == 0, tokens, other), jnp.where(low == 0, other, tokens)])
    w1, w3 = along_z(w0, -1), along_z(w0, 1)
    d0 = copied(prepare_kernel, 512, 8, [d_query, d_key, d_value], scalars=[place])
    d1, d3 = along_x(d0, -1), along_x(d0, 1)
    o0 = other_core(w0)

    (head,) = call(
        head_kernel,
        [shape(512, 192)],
        [d0, proj_query.T, proj_key.T, proj_value.T],
        scalars=[place],
    )
    over_y = dict(axis_index_groups=[[0, 2, 4, 6], [1, 3, 5, 7]], tiled=True)
    heads = lax.all_to_all(head, "tensor", 0, 0, **over_y)
    live = (lengths[y // 2] - y % 2 * 128).reshape(1)
    (outer,) = call(outer_kernel, [shape(4, 96, 128)], [tokens, heads], scalars=[live])
    outer = lax.all_to_all(outer, "tensor", 0, 0, **over_y)
    grads = jnp.sum(outer.reshape(2, 2, 96, 128).astype(F32), axis=1)

    d0, w0, o0, d1, d3, w1, w3, grads = lax.optimization_barrier((d0, w0, o0, d1, d3, w1, w3, grads))
    d2, w2 = along_x(d0, 2), along_z(w0, 2)
    grads = (grads + swap_l(grads)).astype(BF)
    o1, o3 = other_core(w1), other_core(w3)

    far0, far1 = (far1_terms([d0, d1, d3], ws) for ws in ([w0, w1, w3], [o0, o1, o3]))
    grads, _ = lax.optimization_barrier((grads, far1))
    grads = to_all(grads, [[x * 8 + i for i in range(8)] for x in range(4)])
    far0, far1 = along_y(far0, 1), along_y(far1, -1)
    one, three, own = call(
        near1_kernel,
        [shape(2, 128, COLS1)] * 3,
        [d0, d1, d3, w0, o0, w1, o1, w3, o3],
        [pltpu.VMEM((1152, 1280), BF)],
    )
    steps = shape(2, 128, COLS1)
    up, down = call(second_kernel, [steps] * 2, [far0, far1, one, three])
    d2, w2, _, _ = lax.optimization_barrier((d2, w2, up, down))
    up, down = along_y(up, 1), along_y(down, -1)

    o2 = other_core(w2)
    steps = shape(2, 128, COLS2)
    far0, far1, one2, three2, own2 = call(
        stage2_kernel,
        [shape(128, COLS2)] * 2 + [steps] * 3,
        [d0, d1, d3, d2, w0, o0, w1, o1, w3, o3, w2, o2],
        [pltpu.VMEM((1536, 1280), BF)],
    )
    grads, _ = lax.optimization_barrier((grads, far1))
    grads = to_all(grads, [[x * 8 + i for x in range(4)] for i in range(8)])
    far0, far1 = along_y(far0, 1), along_y(far1, -1)

    keep, send = call(third_kernel, [shape(2, TOK, COLS1)] * 2, [own, up, down])
    got = swap_l(send)
    far0, far1, _ = lax.optimization_barrier((far0, far1, send))
    wide, narrow = shape(2, 128, 1024), shape(2, 128, 768)
    up2, down2, up3, down3 = call(
        second2_kernel, [wide, wide, narrow, narrow], [far0, far1, one2, three2]
    )
    up2, down2 = along_y(up2, 1), along_y(down2, -1)
    up3, down3 = along_y(up3, 1), along_y(down3, -1)
    e0, e1, e3 = call(split_kernel, [shape(2, TOK, 768)] * 3, [keep, got])
    up2, down2, _ = lax.optimization_barrier((up2, down2, e1))
    e1, e3 = along_x(e1, 1), along_x(e3, -1)
    keep2, send = call(third_kernel, [shape(2, TOK, 1024)] * 2, [own2, up2, down2])
    got2 = swap_l(send)
    up3, down3, _ = lax.optimization_barrier((up3, down3, send))
    keep3, send = call(
        functools.partial(third_kernel, col=1024), [shape(2, TOK, 768)] * 2, [own2, up3, down3]
    )
    got3 = swap_l(send)
    (f2,) = call(split_kernel, [shape(2, TOK, 1024)], [keep2, got2])
    scores = dot_t(grads.reshape(64, 12288), queries)
    keep3, scores, _ = lax.optimization_barrier((keep3, scores, f2))
    f2 = along_x(f2, 2)
    f0, f1, f3 = call(split_kernel, [shape(2, TOK, 256)] * 3, [keep3, got3])
    f1, f3 = along_x(f1, 1), along_x(f3, -1)

    (grad_hidden,) = call(
        finish_kernel,
        [shape(TOK, 8192)],
        [hidden, gain, e0, e1, e3, f0, f1, f3, f2],
        scalars=[place],
        vmem_limit=VMEM_ALL,
    )
    return scores, grad_hidden


def solution(mesh):
    placed = (
        P(("dp", "tensor"), None),
        P(),
        P("dp", "tensor"),
        P("dp", "tensor"),
        P("dp", "tensor"),
        P("dp", "tensor"),
        P("dp", "tensor"),
        P("dp", "tensor"),
        P("dp"),
        P(),
        P("tensor", None),
        P("tensor", None),
        P("tensor", None),
        P(("dp", "tensor"), None),
    )
    return jax.shard_map(
        local,
        mesh=mesh,
        in_specs=placed,
        out_specs=(P(None, ("dp", "tensor")), P(("dp", "tensor"), None)),
        check_vma=False,
    )
```

```python
import functools

import jax
import jax.numpy as jnp
from jax import lax
from jax.experimental import pallas as pl
from jax.experimental.pallas import tpu as pltpu
from jax.sharding import PartitionSpec as P

EPSILON = 1e-05
BF = jnp.bfloat16
F32 = jnp.float32
VMEM_LIMIT = 48 * 1024 * 1024
VMEM_ALL = 60 * 1024 * 1024

NX, NZ, NC, NY, NL = 4, 4, 2, 4, 2
TOK = 64


def along_x(v, step):
    return lax.ppermute(v, "dp", [(i, (i // 8 + step) % NX * 8 + i % 8) for i in range(32)])


def along_z(v, step):
    return lax.ppermute(
        v, "dp", [(i, i // 8 * 8 + (i // 2 + step) % NZ * 2 + i % 2) for i in range(32)]
    )


def other_core(v):
    return lax.ppermute(v, "dp", [(i, i ^ 1) for i in range(32)])


def along_y(v, step):
    return lax.ppermute(v, "tensor", [(t, (t // 2 + step) % NY * 2 + t % 2) for t in range(8)])


def swap_l(v):
    return lax.ppermute(v, "tensor", [(t, t ^ 1) for t in range(8)])


def prepare_kernel(place, dq, dk, dv, out, held, came, went):
    arrivals, departures = [], []
    for b in range(8):
        low = lax.rem(place[1] + b % 2, 2)
        rows = pl.ds(pl.multiple_of((place[0] + b // 2) % 4 * 128 + low * TOK, TOK), TOK)
        to = slice(b * TOK, b * TOK + TOK)
        for i, (ref, col) in enumerate(((dq, 0), (dk, 1024), (dv, 1152))):
            part = held.at[to, col : col + ref.shape[1]]
            arrivals.append(pltpu.make_async_copy(ref.at[rows], part, came.at[3 * b + i]))
        departures.append(pltpu.make_async_copy(held.at[to], out.at[to], went.at[b]))
    send_on(arrivals, departures)


def side_by_side_kernel(q, k, v, out, held, came, went):
    arrivals, departures = [], []
    for b in range(4):
        rows = slice(b * 64, b * 64 + 64)
        for i, (ref, col) in enumerate(((q, 0), (k, 1024), (v, 1152))):
            part = held.at[rows, col : col + ref.shape[1]]
            arrivals.append(pltpu.make_async_copy(ref.at[rows], part, came.at[3 * b + i]))
        departures.append(pltpu.make_async_copy(held.at[rows], out.at[rows], went.at[b]))
    send_on(arrivals, departures)


def send_on(arrivals, departures):
    for copy in arrivals:
        copy.start()
    for b, copy in enumerate(departures):
        for arrival in arrivals[3 * b : 3 * b + 3]:
            arrival.wait()
        copy.start()
    for copy in departures:
        copy.wait()


def copied(kernel, rows, blocks, args, scalars=()):
    hbm = pl.BlockSpec(memory_space=pltpu.HBM)
    return pl.pallas_call(
        kernel,
        in_specs=[pl.BlockSpec(memory_space=pltpu.SMEM)] * len(scalars) + [hbm] * len(args),
        out_specs=hbm,
        out_shape=shape(rows, 1280),
        scratch_shapes=[
            pltpu.VMEM((rows, 1280), BF),
            pltpu.SemaphoreType.DMA((3 * blocks,)),
            pltpu.SemaphoreType.DMA((blocks,)),
        ],
        compiler_params=pltpu.CompilerParams(vmem_limit_bytes=VMEM_ALL),
        cost_estimate=pl.CostEstimate(flops=1, bytes_accessed=1, transcendentals=0),
    )(*scalars, *args)


def call(kernel, shapes, args, scratch=(), scalars=(), vmem_limit=VMEM_LIMIT, flops=1):
    vmem = pl.BlockSpec(memory_space=pltpu.VMEM)
    return pl.pallas_call(
        kernel,
        in_specs=[pl.BlockSpec(memory_space=pltpu.SMEM)] * len(scalars) + [vmem] * len(args),
        out_specs=[vmem] * len(shapes),
        out_shape=list(shapes),
        scratch_shapes=list(scratch),
        compiler_params=pltpu.CompilerParams(vmem_limit_bytes=vmem_limit),
        cost_estimate=pl.CostEstimate(flops=flops, bytes_accessed=1, transcendentals=0),
    )(*scalars, *args)


def shape(*dims):
    return jax.ShapeDtypeStruct(dims, BF)


def dot_t(left, right):
    return lax.dot_general(left, right, (((1,), (1,)), ((), ())), preferred_element_type=F32)


def head_kernel(place, d, pq, pk, pv, head):
    for m, (p, lo, hi) in enumerate(((pq, 0, 1024), (pk, 1024, 1152), (pv, 1152, 1280))):
        found = dot_t(d[:, lo:hi], p[...]).astype(BF)
        for b in range(8):
            to = (place[0] + b // 2) % 4 * 128 + (place[1] + b % 2) % 2 * TOK
            head[pl.ds(pl.multiple_of(to, TOK), TOK), m * 64 : m * 64 + 64] = found[
                b * TOK : b * TOK + TOK
            ]


def sketch_kernel(hidden, gain, proj, out):
    rows = hidden[...].astype(F32)
    inv = lax.rsqrt(jnp.mean(rows * rows, axis=1, keepdims=True) + EPSILON)
    normed = (rows * inv * gain[...]).astype(BF)
    out[...] = dot_t(normed, proj[...]).astype(BF)


def outer_kernel(live, tokens, heads, out):
    head = heads[0:128].astype(F32)
    for t in range(1, 4):
        head = head + heads[t * 128 : t * 128 + 128].astype(F32)
    at = lax.broadcasted_iota(jnp.int32, (128, 192), 0)
    head = jnp.where(at < live[0], head, 0.0)
    to = lax.broadcasted_iota(jnp.int32, (64, 64), 1)
    source = jnp.where(to < 32, 2 * to, 2 * to - 63)
    pick = (lax.broadcasted_iota(jnp.int32, (64, 64), 0) == source).astype(F32).astype(BF)
    ordered = jnp.dot(tokens[...], pick, preferred_element_type=F32)
    for m in range(3):
        part = lax.dot_general(
            ordered,
            head[:, m * 64 : m * 64 + 64],
            (((0,), (0,)), ((), ())),
            precision=lax.Precision.HIGHEST,
            preferred_element_type=F32,
        ).astype(BF)
        for t in range(4):
            out[t, m * 32 : m * 32 + 32, :64] = part[:32]
            out[t, m * 32 : m * 32 + 32, 64:] = part[32:]


STAGE1 = [(j, r) for j in (0, 1, 3) for r in (0, 1, 3)]
STAGE2 = [(2, r) for r in (0, 1, 3, 2)] + [(j, 2) for j in (0, 1, 3)]
COLS1, COLS2 = 256 * len(STAGE1), 256 * len(STAGE2)


def product(blocks, js, rs, hs, ks, ds, ws, outs, left):
    n = 0
    for j in js:
        for k in ks:
            left[n * 128 : n * 128 + 128] = ds[j][k * 128 : k * 128 + 128]
            n += 1
    for h in hs:
        for r in rs:
            found = dot_t(left[: n * 128], ws[r][h][...]).astype(BF)
            m = 0
            for j in js:
                col = blocks.index((j, r)) * 256
                for k in ks:
                    outs[k][h][:, col : col + 256] = found[m * 128 : m * 128 + 128]
                    m += 1


def far1_kernel(d0, d1, d3, w0, o0, w1, o1, w3, o3, far0, far1, left):
    for n, ref in enumerate((d0, d1, d3)):
        left[n * 128 : n * 128 + 128] = ref[...]
    for out, ws in ((far0, (w0, w1, w3)), (far1, (o0, o1, o3))):
        for i, w in enumerate(ws):
            found = dot_t(left[...], w[...]).astype(BF)
            for n in range(3):
                col = (3 * n + i) * 256
                out[:, col : col + 256] = found[n * 128 : n * 128 + 128]


def far1_terms(ds, ws):
    return pl.pallas_call(
        far1_kernel,
        grid=(1,),
        in_specs=[pl.BlockSpec((128, 1280), lambda i: (2, 0))] * 3
        + [pl.BlockSpec((256, 1280), lambda i: (0, 0))] * 6,
        out_specs=[pl.BlockSpec((128, COLS1), lambda i: (0, 0))] * 2,
        out_shape=[shape(128, COLS1)] * 2,
        scratch_shapes=[pltpu.VMEM((384, 1280), BF)],
        compiler_params=pltpu.CompilerParams(vmem_limit_bytes=VMEM_ALL),
        cost_estimate=pl.CostEstimate(flops=1, bytes_accessed=1, transcendentals=0),
    )(*ds, *ws)


def near1_kernel(d0, d1, d3, w0, o0, w1, o1, w3, o3, one, three, own, left):
    ws = {0: (w0, o0), 1: (w1, o1), 3: (w3, o3)}
    outs = {k: (out.at[0], out.at[1]) for k, out in ((1, one), (3, three), (0, own))}
    product(STAGE1, (0, 1, 3), (0, 1, 3), (0, 1), (1, 3, 0), {0: d0, 1: d1, 3: d3}, ws, outs, left)


def stage2_kernel(d0, d1, d3, d2, w0, o0, w1, o1, w3, o3, w2, o2, far0, far1, one, three, own, left):
    ds = {0: d0, 1: d1, 3: d3, 2: d2}
    ws = {0: (w0, o0), 1: (w1, o1), 3: (w3, o3), 2: (w2, o2)}
    outs = {k: (out.at[0], out.at[1]) for k, out in ((1, one), (3, three), (0, own))}
    outs[2] = (far0, far1)
    product(STAGE2, (2,), (0, 1, 3, 2), (0, 1), (2, 1, 3, 0), ds, ws, outs, left)
    product(STAGE2, (0, 1, 3), (2,), (0, 1), (2, 1, 3, 0), ds, ws, outs, left)


def finish_kernel(place, hidden, gain, e0, e1, e3, f0, f1, f3, f2, out):
    x, z, c = place[2], place[3], place[4]
    rows = hidden[...].astype(F32)
    inv = lax.rsqrt(jnp.mean(rows * rows, axis=1, keepdims=True) + EPSILON)
    places = {(2, r): (f2, i * 256) for i, r in enumerate((0, 1, 3, 2))}
    for j, first, second in ((0, e0, f0), (1, e1, f1), (3, e3, f3)):
        places.update({(j, r): (first, i * 256) for i, r in enumerate((0, 1, 3))})
        places[j, 2] = (second, 0)

    def blocks():
        for (j, r), (ref, col) in places.items():
            for h in range(2):
                block = lax.rem(x + 4 - j, 4) * 8 + lax.rem(z + r, 4) * 2 + lax.rem(c + h, 2)
                cols = pl.ds(pl.multiple_of(block * 256, 256), 256)
                grad = ref[h, :, col : col + 256].astype(F32) * gain[:, cols]
                yield cols, grad, hidden[:, cols].astype(F32) * inv

    total = jnp.zeros((TOK, 256), F32)
    for cols, grad, unit in blocks():
        total += grad * unit
    mean = jnp.sum(total, axis=1, keepdims=True) * (1.0 / 8192)
    for cols, grad, unit in blocks():
        out[:, cols] = (inv * (grad - unit * mean)).astype(BF)


def add(*terms):
    total = terms[0].astype(F32)
    for term in terms[1:]:
        total = total + term.astype(F32)
    return total.astype(BF)


def second_kernel(far_up, far_down, one, three, up, down):
    up[0] = add(one[0], far_up[...])
    up[1] = one[1]
    down[0] = three[0]
    down[1] = add(three[1], far_down[...])


def second2_kernel(far_up, far_down, one, three, up2, down2, up3, down3):
    for up, down, lo, hi in ((up2, down2, 0, 1024), (up3, down3, 1024, 1792)):
        up[0] = add(one[0, :, lo:hi], far_up[:, lo:hi])
        up[1] = one[1, :, lo:hi]
        down[0] = three[0, :, lo:hi]
        down[1] = add(three[1, :, lo:hi], far_down[:, lo:hi])


def third_kernel(own, up, down, keep, send, col=0):
    cols = slice(col, col + up.shape[2])
    keep[...] = add(own[:, :TOK, cols], up[:, :TOK], down[:, :TOK])
    send[...] = add(own[:, TOK:, cols], up[:, TOK:], down[:, TOK:])


def split_kernel(keep, got, *outs):
    col = 0
    for out in outs:
        end = col + out.shape[2]
        out[...] = add(keep[:, :, col:end], got[:, :, col:end])
        col = end


def to_all(v, groups):
    copies = jnp.broadcast_to(v[None], (len(groups[0]), *v.shape))
    v = lax.all_to_all(copies, "dp", 0, 0, axis_index_groups=groups)
    return v.reshape(-1, 96, 128)


def local(
    hidden,
    norm_gain,
    w_query,
    w_key,
    w_value,
    d_query,
    d_key,
    d_value,
    lengths,
    proj_in,
    proj_query,
    proj_key,
    proj_value,
    queries,
):
    dp, tensor = lax.axis_index("dp"), lax.axis_index("tensor")
    x, z, c, y, low = dp // 8, dp // 2 % 4, dp % 2, tensor // 2, tensor % 2
    gain = norm_gain.reshape(1, -1)

    (tokens,) = call(
        sketch_kernel, [shape(TOK, 64)], [hidden, gain, proj_in.T], vmem_limit=VMEM_ALL
    )
    other = swap_l(tokens)

    place = jnp.stack([y, low, x, z, c]).astype(jnp.int32)
    w0 = copied(side_by_side_kernel, 256, 4, [w_query, w_key, w_value])
    w0, other = lax.optimization_barrier((w0, other))
    tokens = jnp.concatenate([jnp.where(low == 0, tokens, other), jnp.where(low == 0, other, tokens)])
    w1, w3 = along_z(w0, -1), along_z(w0, 1)
    d0 = copied(prepare_kernel, 512, 8, [d_query, d_key, d_value], scalars=[place])
    d1, d3 = along_x(d0, -1), along_x(d0, 1)
    o0 = other_core(w0)

    (head,) = call(
        head_kernel,
        [shape(512, 192)],
        [d0, proj_query.T, proj_key.T, proj_value.T],
        scalars=[place],
    )
    over_y = dict(axis_index_groups=[[0, 2, 4, 6], [1, 3, 5, 7]], tiled=True)
    heads = lax.all_to_all(head, "tensor", 0, 0, **over_y)
    live = (lengths[y // 2] - y % 2 * 128).reshape(1)
    (outer,) = call(outer_kernel, [shape(4, 96, 128)], [tokens, heads], scalars=[live])
    outer = lax.all_to_all(outer, "tensor", 0, 0, **over_y)
    grads = jnp.sum(outer.reshape(2, 2, 96, 128).astype(F32), axis=1)

    w1, w3, grads = lax.optimization_barrier((w1, w3, grads))
    o1, o3 = other_core(w1), other_core(w3)
    d0, w0, o0, d1, d3, w1, w3, o1, o3, grads = lax.optimization_barrier(
        (d0, w0, o0, d1, d3, w1, w3, o1, o3, grads)
    )
    d2, w2 = along_x(d0, 2), along_z(w0, 2)
    grads = (grads + swap_l(grads)).astype(BF)

    far0, far1 = far1_terms([d0, d1, d3], [w0, o0, w1, o1, w3, o3])
    grads, _ = lax.optimization_barrier((grads, far1))
    grads = to_all(grads, [[x * 8 + i for i in range(8)] for x in range(4)])
    far0, far1 = along_y(far0, 1), along_y(far1, -1)
    one, three, own = call(
        near1_kernel,
        [shape(2, 128, COLS1)] * 3,
        [d0, d1, d3, w0, o0, w1, o1, w3, o3],
        [pltpu.VMEM((1152, 1280), BF)],
    )
    steps = shape(2, 128, COLS1)
    up, down = call(second_kernel, [steps] * 2, [far0, far1, one, three])
    d2, w2, _, _ = lax.optimization_barrier((d2, w2, up, down))
    up, down = along_y(up, 1), along_y(down, -1)

    first = other_core(w2[:16, :128])
    w2, first = lax.optimization_barrier((w2, first))
    o2 = other_core(w2)
    steps = shape(2, 128, COLS2)
    far0, far1, one2, three2, own2 = call(
        stage2_kernel,
        [shape(128, COLS2)] * 2 + [steps] * 3,
        [d0, d1, d3, d2, w0, o0, w1, o1, w3, o3, w2, o2],
        [pltpu.VMEM((1536, 1280), BF)],
    )
    grads, _ = lax.optimization_barrier((grads, far1))
    grads = to_all(grads, [[x * 8 + i for x in range(4)] for i in range(8)])
    far0, far1 = along_y(far0, 1), along_y(far1, -1)

    keep, send = call(third_kernel, [shape(2, TOK, COLS1)] * 2, [own, up, down])
    got = swap_l(send)
    far0, far1, _ = lax.optimization_barrier((far0, far1, send))
    wide, narrow = shape(2, 128, 1024), shape(2, 128, 768)
    up2, down2, up3, down3 = call(
        second2_kernel, [wide, wide, narrow, narrow], [far0, far1, one2, three2]
    )
    up2, down2 = along_y(up2, 1), along_y(down2, -1)
    up3, down3 = along_y(up3, 1), along_y(down3, -1)
    e0, e1, e3 = call(split_kernel, [shape(2, TOK, 768)] * 3, [keep, got])
    up2, down2, _ = lax.optimization_barrier((up2, down2, e1))
    e1, e3 = along_x(e1, 1), along_x(e3, -1)
    keep2, send = call(third_kernel, [shape(2, TOK, 1024)] * 2, [own2, up2, down2])
    got2 = swap_l(send)
    up3, down3, _ = lax.optimization_barrier((up3, down3, send))
    keep3, send = call(
        functools.partial(third_kernel, col=1024), [shape(2, TOK, 768)] * 2, [own2, up3, down3]
    )
    got3 = swap_l(send)
    (f2,) = call(split_kernel, [shape(2, TOK, 1024)], [keep2, got2])
    scores = dot_t(grads.reshape(64, 12288), queries)
    keep3, scores, _ = lax.optimization_barrier((keep3, scores, f2))
    f2 = along_x(f2, 2)
    f0, f1, f3 = call(split_kernel, [shape(2, TOK, 256)] * 3, [keep3, got3])
    f1, f3 = along_x(f1, 1), along_x(f3, -1)

    (grad_hidden,) = call(
        finish_kernel,
        [shape(TOK, 8192)],
        [hidden, gain, e0, e1, e3, f0, f1, f3, f2],
        scalars=[place],
        vmem_limit=VMEM_ALL,
    )
    return scores, grad_hidden


def solution(mesh):
    placed = (
        P(("dp", "tensor"), None),
        P(),
        P("dp", "tensor"),
        P("dp", "tensor"),
        P("dp", "tensor"),
        P("dp", "tensor"),
        P("dp", "tensor"),
        P("dp", "tensor"),
        P("dp"),
        P(),
        P("tensor", None),
        P("tensor", None),
        P("tensor", None),
        P(("dp", "tensor"), None),
    )
    return jax.shard_map(
        local,
        mesh=mesh,
        in_specs=placed,
        out_specs=(P(None, ("dp", "tensor")), P(("dp", "tensor"), None)),
        check_vma=False,
    )
```

```python
import functools

import jax
import jax.numpy as jnp
from jax import lax
from jax.experimental import pallas as pl
from jax.experimental.pallas import tpu as pltpu
from jax.sharding import PartitionSpec as P

EPSILON = 1e-05
BF = jnp.bfloat16
F32 = jnp.float32
VMEM_LIMIT = 48 * 1024 * 1024
VMEM_LOW = 16 * 1024 * 1024
VMEM_ALL = 60 * 1024 * 1024

NX, NZ, NC, NY, NL = 4, 4, 2, 4, 2
TOK = 64


def along_x(v, step):
    return lax.ppermute(v, "dp", [(i, (i // 8 + step) % NX * 8 + i % 8) for i in range(32)])


def along_z(v, step):
    return lax.ppermute(
        v, "dp", [(i, i // 8 * 8 + (i // 2 + step) % NZ * 2 + i % 2) for i in range(32)]
    )


def other_core(v):
    return lax.ppermute(v, "dp", [(i, i ^ 1) for i in range(32)])


def along_y(v, step):
    return lax.ppermute(v, "tensor", [(t, (t // 2 + step) % NY * 2 + t % 2) for t in range(8)])


def swap_l(v):
    return lax.ppermute(v, "tensor", [(t, t ^ 1) for t in range(8)])


def prepare_kernel(place, dq, dk, dv, out, held, came, went):
    arrivals, departures = [], []
    for b in range(8):
        low = lax.rem(place[1] + b % 2, 2)
        rows = pl.ds(pl.multiple_of((place[0] + b // 2) % 4 * 128 + low * TOK, TOK), TOK)
        to = slice(b * TOK, b * TOK + TOK)
        for i, (ref, col) in enumerate(((dq, 0), (dk, 1024), (dv, 1152))):
            part = held.at[to, col : col + ref.shape[1]]
            arrivals.append(pltpu.make_async_copy(ref.at[rows], part, came.at[3 * b + i]))
        departures.append(pltpu.make_async_copy(held.at[to], out.at[to], went.at[b]))
    send_on(arrivals, departures)


def side_by_side_kernel(q, k, v, out, held, came, went):
    arrivals, departures = [], []
    for b in range(4):
        rows = slice(b * 64, b * 64 + 64)
        for i, (ref, col) in enumerate(((q, 0), (k, 1024), (v, 1152))):
            part = held.at[rows, col : col + ref.shape[1]]
            arrivals.append(pltpu.make_async_copy(ref.at[rows], part, came.at[3 * b + i]))
        departures.append(pltpu.make_async_copy(held.at[rows], out.at[rows], went.at[b]))
    send_on(arrivals, departures)


def send_on(arrivals, departures):
    for copy in arrivals:
        copy.start()
    for b, copy in enumerate(departures):
        for arrival in arrivals[3 * b : 3 * b + 3]:
            arrival.wait()
        copy.start()
    for copy in departures:
        copy.wait()


def copied(kernel, rows, blocks, args, scalars=()):
    hbm = pl.BlockSpec(memory_space=pltpu.HBM)
    return pl.pallas_call(
        kernel,
        in_specs=[pl.BlockSpec(memory_space=pltpu.SMEM)] * len(scalars) + [hbm] * len(args),
        out_specs=hbm,
        out_shape=shape(rows, 1280),
        scratch_shapes=[
            pltpu.VMEM((rows, 1280), BF),
            pltpu.SemaphoreType.DMA((3 * blocks,)),
            pltpu.SemaphoreType.DMA((blocks,)),
        ],
        compiler_params=pltpu.CompilerParams(vmem_limit_bytes=VMEM_ALL),
        cost_estimate=pl.CostEstimate(flops=1, bytes_accessed=1, transcendentals=0),
    )(*scalars, *args)


def call(kernel, shapes, args, scratch=(), scalars=(), vmem_limit=VMEM_LIMIT, flops=1):
    vmem = pl.BlockSpec(memory_space=pltpu.VMEM)
    return pl.pallas_call(
        kernel,
        in_specs=[pl.BlockSpec(memory_space=pltpu.SMEM)] * len(scalars) + [vmem] * len(args),
        out_specs=[vmem] * len(shapes),
        out_shape=list(shapes),
        scratch_shapes=list(scratch),
        compiler_params=pltpu.CompilerParams(vmem_limit_bytes=vmem_limit),
        cost_estimate=pl.CostEstimate(flops=flops, bytes_accessed=1, transcendentals=0),
    )(*scalars, *args)


def shape(*dims):
    return jax.ShapeDtypeStruct(dims, BF)


def dot_t(left, right):
    return lax.dot_general(left, right, (((1,), (1,)), ((), ())), preferred_element_type=F32)


def head_kernel(place, d, pq, pk, pv, head):
    for m, (p, lo, hi) in enumerate(((pq, 0, 1024), (pk, 1024, 1152), (pv, 1152, 1280))):
        found = dot_t(d[:, lo:hi], p[...]).astype(BF)
        for b in range(8):
            to = (place[0] + b // 2) % 4 * 128 + (place[1] + b % 2) % 2 * TOK
            head[pl.ds(pl.multiple_of(to, TOK), TOK), m * 64 : m * 64 + 64] = found[
                b * TOK : b * TOK + TOK
            ]


def sketch_kernel(hidden, gain, proj, out):
    rows = hidden[...].astype(F32)
    inv = lax.rsqrt(jnp.mean(rows * rows, axis=1, keepdims=True) + EPSILON)
    normed = (rows * inv * gain[...]).astype(BF)
    out[...] = dot_t(normed, proj[...]).astype(BF)


def outer_kernel(live, tokens, heads, out):
    head = heads[0:128].astype(F32)
    for t in range(1, 4):
        head = head + heads[t * 128 : t * 128 + 128].astype(F32)
    at = lax.broadcasted_iota(jnp.int32, (128, 192), 0)
    head = jnp.where(at < live[0], head, 0.0)
    to = lax.broadcasted_iota(jnp.int32, (64, 64), 1)
    source = jnp.where(to < 32, 2 * to, 2 * to - 63)
    pick = (lax.broadcasted_iota(jnp.int32, (64, 64), 0) == source).astype(F32).astype(BF)
    ordered = jnp.dot(tokens[...], pick, preferred_element_type=F32)
    for m in range(3):
        part = lax.dot_general(
            ordered,
            head[:, m * 64 : m * 64 + 64],
            (((0,), (0,)), ((), ())),
            precision=lax.Precision.HIGHEST,
            preferred_element_type=F32,
        ).astype(BF)
        for t in range(4):
            out[t, m * 32 : m * 32 + 32, :64] = part[:32]
            out[t, m * 32 : m * 32 + 32, 64:] = part[32:]


STAGE1 = [(j, r) for j in (0, 1, 3) for r in (0, 1, 3)]
STAGE2 = [(2, r) for r in (0, 1, 3, 2)] + [(j, 2) for j in (0, 1, 3)]
COLS1, COLS2 = 256 * len(STAGE1), 256 * len(STAGE2)


def product(blocks, js, rs, hs, ks, ds, ws, outs, left):
    n = 0
    for j in js:
        for k in ks:
            left[n * 128 : n * 128 + 128] = ds[j][k * 128 : k * 128 + 128]
            n += 1
    for h in hs:
        for r in rs:
            found = dot_t(left[: n * 128], ws[r][h][...]).astype(BF)
            m = 0
            for j in js:
                col = blocks.index((j, r)) * 256
                for k in ks:
                    outs[k][h][:, col : col + 256] = found[m * 128 : m * 128 + 128]
                    m += 1


def far1_kernel(d0, d1, d3, w0, o0, w1, o1, w3, o3, far0, far1, left):
    for n, ref in enumerate((d0, d1, d3)):
        left[n * 128 : n * 128 + 128] = ref[...]
    for out, ws in ((far0, (w0, w1, w3)), (far1, (o0, o1, o3))):
        for i, w in enumerate(ws):
            found = dot_t(left[...], w[...]).astype(BF)
            for n in range(3):
                col = (3 * n + i) * 256
                out[:, col : col + 256] = found[n * 128 : n * 128 + 128]


def far1_terms(ds, ws):
    return pl.pallas_call(
        far1_kernel,
        grid=(1,),
        in_specs=[pl.BlockSpec((128, 1280), lambda i: (2, 0))] * 3
        + [pl.BlockSpec((256, 1280), lambda i: (0, 0))] * 6,
        out_specs=[pl.BlockSpec((128, COLS1), lambda i: (0, 0))] * 2,
        out_shape=[shape(128, COLS1)] * 2,
        scratch_shapes=[pltpu.VMEM((384, 1280), BF)],
        compiler_params=pltpu.CompilerParams(vmem_limit_bytes=VMEM_ALL),
        cost_estimate=pl.CostEstimate(flops=1, bytes_accessed=1, transcendentals=0),
    )(*ds, *ws)


def near1_kernel(d0, d1, d3, w0, o0, w1, o1, w3, o3, one, three, own, left):
    ws = {0: (w0, o0), 1: (w1, o1), 3: (w3, o3)}
    outs = {k: (out.at[0], out.at[1]) for k, out in ((1, one), (3, three), (0, own))}
    product(STAGE1, (0, 1, 3), (0, 1, 3), (0, 1), (1, 3, 0), {0: d0, 1: d1, 3: d3}, ws, outs, left)


def stage2_kernel(d0, d1, d3, d2, w0, o0, w1, o1, w3, o3, w2, o2, far0, far1, one, three, own, left):
    ds = {0: d0, 1: d1, 3: d3, 2: d2}
    ws = {0: (w0, o0), 1: (w1, o1), 3: (w3, o3), 2: (w2, o2)}
    outs = {k: (out.at[0], out.at[1]) for k, out in ((1, one), (3, three), (0, own))}
    outs[2] = (far0, far1)
    product(STAGE2, (2,), (0, 1, 3, 2), (0, 1), (2, 1, 3, 0), ds, ws, outs, left)
    product(STAGE2, (0, 1, 3), (2,), (0, 1), (2, 1, 3, 0), ds, ws, outs, left)


def finish_kernel(place, hidden, gain, e0, e1, e3, f0, f1, f3, f2, out):
    x, z, c = place[2], place[3], place[4]
    rows = hidden[...].astype(F32)
    inv = lax.rsqrt(jnp.mean(rows * rows, axis=1, keepdims=True) + EPSILON)
    places = {(2, r): (f2, i * 256) for i, r in enumerate((0, 1, 3, 2))}
    for j, first, second in ((0, e0, f0), (1, e1, f1), (3, e3, f3)):
        places.update({(j, r): (first, i * 256) for i, r in enumerate((0, 1, 3))})
        places[j, 2] = (second, 0)

    def blocks():
        for (j, r), (ref, col) in places.items():
            for h in range(2):
                block = lax.rem(x + 4 - j, 4) * 8 + lax.rem(z + r, 4) * 2 + lax.rem(c + h, 2)
                cols = pl.ds(pl.multiple_of(block * 256, 256), 256)
                grad = ref[h, :, col : col + 256].astype(F32) * gain[:, cols]
                yield cols, grad, hidden[:, cols].astype(F32) * inv

    total = jnp.zeros((TOK, 256), F32)
    for cols, grad, unit in blocks():
        total += grad * unit
    mean = jnp.sum(total, axis=1, keepdims=True) * (1.0 / 8192)
    for cols, grad, unit in blocks():
        out[:, cols] = (inv * (grad - unit * mean)).astype(BF)


def add(*terms):
    total = terms[0].astype(F32)
    for term in terms[1:]:
        total = total + term.astype(F32)
    return total.astype(BF)


def second_kernel(far_up, far_down, one, three, up, down):
    up[0] = add(one[0], far_up[...])
    up[1] = one[1]
    down[0] = three[0]
    down[1] = add(three[1], far_down[...])


def second2_kernel(far_up, far_down, one, three, up2, down2, up3, down3):
    for up, down, lo, hi in ((up2, down2, 0, 1024), (up3, down3, 1024, 1792)):
        up[0] = add(one[0, :, lo:hi], far_up[:, lo:hi])
        up[1] = one[1, :, lo:hi]
        down[0] = three[0, :, lo:hi]
        down[1] = add(three[1, :, lo:hi], far_down[:, lo:hi])


def third_kernel(own, up, down, keep, send, col=0):
    cols = slice(col, col + up.shape[2])
    keep[...] = add(own[:, :TOK, cols], up[:, :TOK], down[:, :TOK])
    send[...] = add(own[:, TOK:, cols], up[:, TOK:], down[:, TOK:])


def split_kernel(keep, got, *outs):
    col = 0
    for out in outs:
        end = col + out.shape[2]
        out[...] = add(keep[:, :, col:end], got[:, :, col:end])
        col = end


def to_all(v, groups):
    copies = jnp.broadcast_to(v[None], (len(groups[0]), *v.shape))
    v = lax.all_to_all(copies, "dp", 0, 0, axis_index_groups=groups)
    return v.reshape(-1, 96, 128)


def local(
    hidden,
    norm_gain,
    w_query,
    w_key,
    w_value,
    d_query,
    d_key,
    d_value,
    lengths,
    proj_in,
    proj_query,
    proj_key,
    proj_value,
    queries,
):
    dp, tensor = lax.axis_index("dp"), lax.axis_index("tensor")
    x, z, c, y, low = dp // 8, dp // 2 % 4, dp % 2, tensor // 2, tensor % 2
    gain = norm_gain.reshape(1, -1)

    (tokens,) = call(
        sketch_kernel, [shape(TOK, 64)], [hidden, gain, proj_in.T], vmem_limit=VMEM_ALL
    )
    other = swap_l(tokens)

    place = jnp.stack([y, low, x, z, c]).astype(jnp.int32)
    w0 = copied(side_by_side_kernel, 256, 4, [w_query, w_key, w_value])
    w0, other = lax.optimization_barrier((w0, other))
    tokens = jnp.concatenate([jnp.where(low == 0, tokens, other), jnp.where(low == 0, other, tokens)])
    w1, w3 = along_z(w0, -1), along_z(w0, 1)
    d0 = copied(prepare_kernel, 512, 8, [d_query, d_key, d_value], scalars=[place])
    d1, d3 = along_x(d0, -1), along_x(d0, 1)
    o0 = other_core(w0)

    (head,) = call(
        head_kernel,
        [shape(512, 192)],
        [d0, proj_query.T, proj_key.T, proj_value.T],
        scalars=[place],
    )
    over_y = dict(axis_index_groups=[[0, 2, 4, 6], [1, 3, 5, 7]], tiled=True)
    heads = lax.all_to_all(head, "tensor", 0, 0, **over_y)
    live = (lengths[y // 2] - y % 2 * 128).reshape(1)
    (outer,) = call(outer_kernel, [shape(4, 96, 128)], [tokens, heads], scalars=[live])
    outer = lax.all_to_all(outer, "tensor", 0, 0, **over_y)
    grads = jnp.sum(outer.reshape(2, 2, 96, 128).astype(F32), axis=1)

    w1, w3, grads = lax.optimization_barrier((w1, w3, grads))
    o1, o3 = other_core(w1), other_core(w3)
    d0, w0, o0, d1, d3, w1, w3, o1, o3, grads = lax.optimization_barrier(
        (d0, w0, o0, d1, d3, w1, w3, o1, o3, grads)
    )
    d2, w2 = along_x(d0, 2), along_z(w0, 2)
    grads = (grads + swap_l(grads)).astype(BF)

    far0, far1 = far1_terms([d0, d1, d3], [w0, o0, w1, o1, w3, o3])
    grads, _ = lax.optimization_barrier((grads, far1))
    grads = to_all(grads, [[x * 8 + i for i in range(8)] for x in range(4)])
    far0, far1 = along_y(far0, 1), along_y(far1, -1)
    one, three, own = call(
        near1_kernel,
        [shape(2, 128, COLS1)] * 3,
        [d0, d1, d3, w0, o0, w1, o1, w3, o3],
        [pltpu.VMEM((1152, 1280), BF)],
        vmem_limit=VMEM_LOW,
    )
    steps = shape(2, 128, COLS1)
    up, down = call(second_kernel, [steps] * 2, [far0, far1, one, three])
    d2, w2, _, _ = lax.optimization_barrier((d2, w2, up, down))
    up, down = along_y(up, 1), along_y(down, -1)

    first = other_core(w2[:16, :128])
    w2, first = lax.optimization_barrier((w2, first))
    o2 = other_core(w2)
    steps = shape(2, 128, COLS2)
    far0, far1, one2, three2, own2 = call(
        stage2_kernel,
        [shape(128, COLS2)] * 2 + [steps] * 3,
        [d0, d1, d3, d2, w0, o0, w1, o1, w3, o3, w2, o2],
        [pltpu.VMEM((1536, 1280), BF)],
        vmem_limit=VMEM_ALL,
    )
    grads, _ = lax.optimization_barrier((grads, far1))
    grads = to_all(grads, [[x * 8 + i for x in range(4)] for i in range(8)])
    far0, far1 = along_y(far0, 1), along_y(far1, -1)

    keep, send = call(third_kernel, [shape(2, TOK, COLS1)] * 2, [own, up, down])
    got = swap_l(send)
    far0, far1, _ = lax.optimization_barrier((far0, far1, send))
    wide, narrow = shape(2, 128, 1024), shape(2, 128, 768)
    up2, down2, up3, down3 = call(
        second2_kernel, [wide, wide, narrow, narrow], [far0, far1, one2, three2]
    )
    up2, down2 = along_y(up2, 1), along_y(down2, -1)
    up3, down3 = along_y(up3, 1), along_y(down3, -1)
    e0, e1, e3 = call(split_kernel, [shape(2, TOK, 768)] * 3, [keep, got])
    up2, down2, _ = lax.optimization_barrier((up2, down2, e1))
    e1, e3 = along_x(e1, 1), along_x(e3, -1)
    keep2, send = call(third_kernel, [shape(2, TOK, 1024)] * 2, [own2, up2, down2])
    got2 = swap_l(send)
    up3, down3, _ = lax.optimization_barrier((up3, down3, send))
    keep3, send = call(
        functools.partial(third_kernel, col=1024), [shape(2, TOK, 768)] * 2, [own2, up3, down3]
    )
    got3 = swap_l(send)
    (f2,) = call(split_kernel, [shape(2, TOK, 1024)], [keep2, got2])
    scores = dot_t(grads.reshape(64, 12288), queries)
    keep3, scores, _ = lax.optimization_barrier((keep3, scores, f2))
    f2 = along_x(f2, 2)
    f0, f1, f3 = call(split_kernel, [shape(2, TOK, 256)] * 3, [keep3, got3])
    f1, f3 = along_x(f1, 1), along_x(f3, -1)

    (grad_hidden,) = call(
        finish_kernel,
        [shape(TOK, 8192)],
        [hidden, gain, e0, e1, e3, f0, f1, f3, f2],
        scalars=[place],
        vmem_limit=VMEM_ALL,
    )
    return scores, grad_hidden


def solution(mesh):
    placed = (
        P(("dp", "tensor"), None),
        P(),
        P("dp", "tensor"),
        P("dp", "tensor"),
        P("dp", "tensor"),
        P("dp", "tensor"),
        P("dp", "tensor"),
        P("dp", "tensor"),
        P("dp"),
        P(),
        P("tensor", None),
        P("tensor", None),
        P("tensor", None),
        P(("dp", "tensor"), None),
    )
    return jax.shard_map(
        local,
        mesh=mesh,
        in_specs=placed,
        out_specs=(P(None, ("dp", "tensor")), P(("dp", "tensor"), None)),
        check_vma=False,
    )
```
